32 devices in a mesh: rows: 8 (over y, x, core), kc: 4 (over z).
Axes of the slice: x: 2, y: 2, z: 4, core: 2. Of those that a mesh axis runs over, the one named last changes fastest.
Arguments:
- inputs: bfloat16 [4, 2048, 768], P(None, ('rows', 'kc')), may hold values from -6 to 6
- w_query: bfloat16 [768, 768], replicated, may hold values from -0.4375 to 0.4375
- w_key: bfloat16 [768, 768], replicated, may hold values from -0.21875 to 0.21875
- w_value: bfloat16 [768, 768], replicated, may hold values from -0.21875 to 0.21875
- w_out: bfloat16 [768, 768], replicated, may hold values from -1.25 to 1.25
- w_up: bfloat16 [768, 3072], replicated, may hold values from -0.21875 to 0.21875
- w_down: bfloat16 [3072, 768], replicated, may hold values from -0.109375 to 0.109375
- gain_attn: float32 [768], replicated, may hold values from 0.5 to 1.5
- gain_ffn: float32 [768], replicated, may hold values from 0.5 to 1.5
- proj_e: bfloat16 [256, 256], P(None, 'kc'), may hold values from -0.375 to 0.375
- lengths: int32 [4, 8], P(None, 'rows'), may hold values from 16 to 256, as said below
- cotangent: bfloat16 [4, 2048, 768], P(None, ('rows', 'kc')), may hold values from -6 to 6
Outputs:
- output: bfloat16 [4, 2048, 768], P(None, ('rows', 'kc'))
- grad_inputs: bfloat16 [4, 2048, 768], P(None, ('rows', 'kc'))
- grad_query: float32 [768, 768], P('rows', 'kc')
- grad_key: float32 [768, 768], P('rows', 'kc')
- grad_value: float32 [768, 768], P('rows', 'kc')
- grad_out: float32 [768, 768], P('rows', 'kc')
- grad_up: float32 [768, 3072], P('rows', 'kc')
- grad_down: float32 [3072, 768], P('rows', 'kc')
- grad_gain_attn: float32 [768], P('rows')
- grad_gain_ffn: float32 [768], P('rows')
- grad_proj_e: float32 [256, 256], P('rows', 'kc')
The draws below stay inside these ranges and needn't reach their ends.
Inputs may be any that keep to these rules, and one draw needn't show every extreme that they name: `lengths`: for every sequence index g, one micro-batch holds a sequence of the full 256 positions.
All inputs are finite; a program needn't handle non-finite values.
Results may differ from the reference program's by a relative error of at most 0.018.
Values may be sent and summed in bfloat16 or wider, within the bound.
No kernel may reach another device: no remote copies, remote signals or barrier semaphores. Data moves between devices by JAX's collectives and lax.ppermute only.
A program may use at most 192 MiB of HBM per device.

```python
import jax
import jax.numpy as jnp
from jax import lax

D = 768
HEADS = 12
HEAD = 64
FF = 3072
KDIM = 256
MB = 4
SEQ = 256
TOKENS = 2048
N_ROWS = 8


def draw_lengths(key, part):
    first_key = jax.random.fold_in(key, 11)
    second_key = jax.random.fold_in(key, 23)
    drawn = jax.random.randint(first_key, (MB, N_ROWS), SEQ // 16, SEQ + 1)
    full_batch = jax.random.randint(second_key, (1, N_ROWS), 0, MB)
    batch_index = jnp.arange(MB)[:, None]
    return jnp.where(batch_index == full_batch, SEQ, drawn).astype(jnp.int32)


def shard_levels(key, shape, split, least, largest):
    factor_of = 1.0
    for position, parts in split:
        heights = jax.random.uniform(jax.random.fold_in(jax.random.fold_in(key, 6), position), (parts,), jnp.float32, least / len(split), largest / len(split))
        factor_of = factor_of * jnp.repeat(jnp.exp(heights), shape[position] // parts).reshape((-1,) + (1,) * (len(shape) - 1 - position))
    return factor_of


def normal_values(stream_key, extent, spread, limit, pieces=(), kind=jnp.bfloat16):
    values = spread * jax.random.normal(stream_key, extent, jnp.float32)
    if pieces:
        values = values * shard_levels(stream_key, extent, pieces, -0.22, 0.18)
    return jnp.clip(values, -limit, limit).astype(kind)


def setup_inputs(seed: int = 0) -> dict:
    seeds = jax.random.split(jax.random.key(seed), 13)
    return {
        "inputs": normal_values(seeds[0], (MB, TOKENS, D), 1.0, 6.0, ((1, 32),)),
        "w_query": normal_values(seeds[1], (D, D), (D // 4) ** -0.5, 0.4375),
        "w_key": normal_values(seeds[2], (D, D), D ** -0.5, 0.21875),
        "w_value": normal_values(seeds[3], (D, D), D ** -0.5, 0.21875),
        "w_out": normal_values(seeds[4], (D, D), (D // 32) ** -0.5, 1.25),
        "w_up": normal_values(seeds[5], (D, FF), D ** -0.5, 0.21875),
        "w_down": normal_values(seeds[6], (FF, D), FF ** -0.5, 0.109375),
        "gain_attn": jnp.clip(1.0 + 0.1 * jax.random.normal(seeds[7], (D,), jnp.float32), 0.5, 1.5),
        "gain_ffn": jnp.clip(1.0 + 0.1 * jax.random.normal(seeds[8], (D,), jnp.float32), 0.5, 1.5),
        "proj_e": normal_values(seeds[9], (SEQ, KDIM), SEQ ** -0.5, 0.375, ((1, 4),)),
        "lengths": draw_lengths(jax.random.fold_in(seeds[12], 71), 0),
        "cotangent": normal_values(seeds[11], (MB, TOKENS, D), 1.0, 6.0, ((1, 32),)),
    }


@jax.custom_vjp
def low(v):
    return lax.optimization_barrier(v.astype(jnp.bfloat16)).astype(jnp.float32)

@jax.custom_vjp
def low_back(v):
    return v

def low_keep(v):
    return (low(v), None)

def low_pass(kept, grad):
    return (grad,)

def back_keep(v):
    return (v, None)

def back_low(kept, grad):
    return (low(grad),)
low.defvjp(low_keep, low_pass)
low_back.defvjp(back_keep, back_low)
highest = lax.Precision.HIGHEST

def normed(values, norm_gain):
    row_mean = lax.optimization_barrier(jnp.mean(values, axis=-1, keepdims=True))
    centred = values - row_mean
    return centred * lax.rsqrt(lax.optimization_barrier(jnp.mean(centred * centred, axis=-1, keepdims=True)) + 1e-05) * norm_gain

def matmul_all(left, right):
    return jnp.einsum('mta,ab->mtb', left, right, precision=highest)

def reference(inputs, w_query, w_key, w_value, w_out, w_up, w_down, gain_attn, gain_ffn, proj_e, lengths, cotangent):
    scale = HEAD ** (-0.5)
    count = MB * N_ROWS
    seq_lens = lengths.reshape(count).astype(jnp.int32)

    def layer(x_all, wq, wk, wv, wo, wu, wd, ga, gf, proj):
        h_low = low(normed(x_all, ga))
        query = low_back(low(matmul_all(h_low, wq)))
        key_all = low_back(low(matmul_all(h_low, wk)))
        value_all = low_back(low(matmul_all(h_low, wv)))

        def one_seq(item):
            q_seq, k_seq, v_seq, seq_len = item
            valid = (jnp.arange(SEQ) < seq_len).astype(jnp.float32)
            e_masked = proj * valid[:, None]
            k_comp = low_back(low(jnp.einsum('tk,td->kd', e_masked, k_seq, precision=highest)))
            v_comp = low_back(low(jnp.einsum('tk,td->kd', e_masked, v_seq, precision=highest)))
            q_heads = q_seq.reshape(SEQ, HEADS, HEAD)
            scores = low_back(jnp.einsum('qhd,khd->hqk', q_heads, k_comp.reshape(KDIM, HEADS, HEAD), precision=highest) * scale)
            p_low = low(jax.nn.softmax(scores, axis=-1))
            attended = jnp.einsum('hqk,khd->qhd', p_low, v_comp.reshape(KDIM, HEADS, HEAD), precision=highest)
            return attended.reshape(SEQ, D)
        attended = lax.map(jax.checkpoint(one_seq), (query.reshape(count, SEQ, D), key_all.reshape(count, SEQ, D), value_all.reshape(count, SEQ, D), seq_lens))
        attended = low_back(low(attended.reshape(MB, TOKENS, D)))
        mid = x_all + low_back(matmul_all(attended, wo))
        h2_low = low(normed(mid, gf))
        up_rows = low_back(matmul_all(h2_low, wu))
        act_low = low(jax.nn.gelu(up_rows))
        return mid + matmul_all(act_low, wd)
    primals = (inputs.astype(jnp.float32), w_query.astype(jnp.float32), w_key.astype(jnp.float32), w_value.astype(jnp.float32), w_out.astype(jnp.float32), w_up.astype(jnp.float32), w_down.astype(jnp.float32), gain_attn.astype(jnp.float32), gain_ffn.astype(jnp.float32), proj_e.astype(jnp.float32))
    result, pullback = jax.vjp(layer, *primals)
    grads = pullback(cotangent.astype(jnp.float32))
    return (result.astype(jnp.bfloat16), grads[0].astype(jnp.bfloat16), grads[1], grads[2], grads[3], grads[4], grads[5], grads[6], grads[7], grads[8], grads[9])
```

```python
import math

import jax
import jax.numpy as jnp
from jax import lax
from jax.sharding import PartitionSpec as P

HEAD = 64
BF = jnp.bfloat16
F32 = jnp.float32


def normed(values):
    centred = values - jnp.mean(values, axis=-1, keepdims=True)
    rstd = lax.rsqrt(jnp.mean(centred * centred, axis=-1, keepdims=True) + 1e-05)
    return centred * rstd, rstd


def norm_back(n, rstd, gain, d):
    dc = d * gain
    return rstd * (
        dc - jnp.mean(dc, axis=-1, keepdims=True) - n * jnp.mean(dc * n, axis=-1, keepdims=True)
    )


def mm(left, right):
    return jnp.dot(left, right, preferred_element_type=F32)


def mm_t(left, right):
    return jnp.einsum("ta,ba->tb", left, right, preferred_element_type=F32)


def t_mm(left, right):
    return jnp.einsum("ta,tb->ab", left, right, preferred_element_type=F32)


class Grid:
    def __init__(self, n_rows, n_kc):
        self.n_rows, self.n_kc = n_rows, n_kc
        self.nc = 2 if n_rows % 2 == 0 else 1
        plane = n_rows // self.nc
        self.nx = next(d for d in range(math.isqrt(plane), 0, -1) if plane % d == 0)
        self.ny = plane // self.nx
        row = lax.axis_index("rows")
        self.c = row % self.nc
        self.x = (row // self.nc) % self.nx
        self.y = row // (self.nc * self.nx)
        self.z = lax.axis_index("kc")

    def send(self, value, axis, shift):
        if axis == "z":
            n = self.n_kc
            return lax.ppermute(value, "kc", [(i, (i + shift) % n) for i in range(n)])
        pairs = []
        for i in range(self.n_rows):
            c, x, y = i % self.nc, (i // self.nc) % self.nx, i // (self.nc * self.nx)
            if axis == "c":
                c = (c + shift) % self.nc
            elif axis == "x":
                x = (x + shift) % self.nx
            else:
                y = (y + shift) % self.ny
            pairs.append((i, (y * self.nx + x) * self.nc + c))
        return lax.ppermute(value, "rows", pairs)

    def scatter_sum(self, value, dim, axis):
        n = {"c": self.nc, "x": self.nx, "y": self.ny, "z": self.n_kc}[axis]
        me = {"c": self.c, "x": self.x, "y": self.y, "z": self.z}[axis]
        total = lax.dynamic_index_in_dim(value, me, dim, keepdims=False).astype(F32)
        for shift in range(1, n):
            block = lax.dynamic_index_in_dim(value, (me + shift) % n, dim, keepdims=False)
            total = total + self.send(block, axis, shift).astype(F32)
        return total


def reduce_grad(grid, value, low=True):
    kind = BF if low else F32
    half = value.shape[2] // 2
    if half % 16:
        parts = ((value, "x"),)
    else:
        parts = ((value[:, :, :half], "x"), (value[:, :, half:], "y"))
    done = []
    for part, first in parts:
        part = part.astype(kind)
        if first == "x":
            part = grid.scatter_sum(part, 1, "x").astype(kind)
            part = grid.scatter_sum(part, 0, "y").astype(kind)
        else:
            part = grid.scatter_sum(part, 0, "y").astype(kind)
            part = grid.scatter_sum(part, 0, "x").astype(kind)
        done.append(grid.scatter_sum(part, 1, "z"))
    return jnp.concatenate(done, axis=0)


def local(
    inputs,
    w_query,
    w_key,
    w_value,
    w_out,
    w_up,
    w_down,
    gain_attn,
    gain_ffn,
    proj_e,
    lengths,
    cotangent,
):
    batches, t, width = inputs.shape
    heads = width // HEAD
    ff = w_up.shape[1]
    scale = HEAD ** (-0.5)
    n_rows, n_kc = lax.axis_size("rows"), lax.axis_size("kc")
    grid = Grid(n_rows, n_kc)
    share = n_kc // batches
    seq_len = proj_e.shape[0]
    mine = batches * t
    my_batch, my_part = grid.z // share, grid.z % share
    lane, part = grid.z % batches, grid.z // batches

    def reorder(got, first):
        stacked = jnp.stack(got)
        return jnp.stack(
            [
                lax.dynamic_index_in_dim(stacked, (first - i) % batches, 0, keepdims=False)
                for i in range(batches)
            ]
        )

    def gather_seq(v):
        got = []
        for j in range(batches):
            block = lax.dynamic_index_in_dim(v, (lane + j) % batches, 0, keepdims=False)
            pairs = [
                (i, ((i % batches + j) % batches) * share + i // batches) for i in range(n_kc)
            ]
            got.append(block if all(a == b for a, b in pairs) else lax.ppermute(block, "kc", pairs))
        return reorder(got, my_batch).reshape(mine, width)

    def spread_seq(v):
        blocks = v.reshape(batches, t, width)
        got = []
        for j in range(batches):
            block = lax.dynamic_index_in_dim(blocks, (my_batch - j) % batches, 0, keepdims=False)
            pairs = [
                (((i % batches + j) % batches) * share + i // batches, i) for i in range(n_kc)
            ]
            got.append(block if all(a == b for a, b in pairs) else lax.ppermute(block, "kc", pairs))
        return reorder(got[:1] + got[:0:-1], lane + batches).reshape(inputs.shape)

    def seq_sum(v):
        if share == 1:
            return v
        groups = [[b * share + p for p in range(share)] for b in range(batches)]
        return lax.psum(v, "kc", axis_index_groups=groups)

    x_low = gather_seq(inputs)
    e_t = lax.all_gather(proj_e.T, "kc", axis=0, tiled=True)
    dy = gather_seq(cotangent)
    e_t = lax.dynamic_slice_in_dim(e_t, my_part * mine, mine, 1)
    length = lax.dynamic_index_in_dim(lengths, my_batch, 0, keepdims=False)[0]
    valid = (my_part * mine + jnp.arange(mine)) < length
    e_mask = jnp.where(valid[None, :], e_t, jnp.zeros_like(e_t))

    x = x_low.astype(F32)
    n1, r1 = normed(x)
    h = (n1 * gain_attn).astype(BF)
    query, key, value = (mm(h, w).astype(BF) for w in (w_query, w_key, w_value))
    k_comp = seq_sum(mm(e_mask, key)).astype(BF)
    v_comp = seq_sum(mm(e_mask, value)).astype(BF)
    q_h = query.reshape(mine, heads, HEAD)
    kc_h = k_comp.reshape(-1, heads, HEAD)
    vc_h = v_comp.reshape(-1, heads, HEAD)
    scores = jnp.einsum("qhd,khd->hqk", q_h, kc_h, preferred_element_type=F32) * scale
    probs = jax.nn.softmax(scores, axis=-1)
    p_low = probs.astype(BF)
    attended = (
        jnp.einsum("hqk,khd->qhd", p_low, vc_h, preferred_element_type=F32)
        .reshape(mine, width)
        .astype(BF)
    )
    mid = x + mm(attended, w_out)
    n2, r2 = normed(mid)
    h2 = (n2 * gain_ffn).astype(BF)
    up = mm(h2, w_up)
    act = jax.nn.gelu(up).astype(BF)
    output = spread_seq((mid + mm(act, w_down)).astype(BF))

    nc, nx, ny = grid.nc, grid.nx, grid.ny

    def by_core(v):
        v = v.reshape(mine, ny * nx, nc, -1)
        own = lax.dynamic_index_in_dim(v, grid.c, 2, keepdims=False)
        other = lax.dynamic_index_in_dim(v, nc - 1 - grid.c, 2, keepdims=False)
        return own.reshape(mine, -1), other.reshape(mine, -1)

    def pair_grad(split, whole):
        own, other = by_core(split)
        return t_mm(own, whole) + t_mm(grid.send(other, "c", 1), grid.send(whole, "c", 1))

    g_down = pair_grad(act, dy)
    g_down = reduce_grad(grid, g_down.reshape(ny, nx, ff // n_rows, n_kc, width // n_kc))
    d_act = mm_t(dy, w_down)
    d_up = jax.vjp(jax.nn.gelu, up)[1](d_act)[0].astype(BF)
    g_up = pair_grad(h2, d_up)
    g_up = reduce_grad(grid, g_up.reshape(ny, nx, width // n_rows, n_kc, ff // n_kc))
    d_h2 = mm_t(d_up, w_up)
    gg_ffn = jnp.sum(d_h2 * n2, axis=0)
    d_mid = dy.astype(F32) + norm_back(n2, r2, gain_ffn, d_h2)
    d_attn = d_mid.astype(BF)
    d_att = mm_t(d_attn, w_out).astype(BF)
    do_h = d_att.reshape(mine, heads, HEAD)
    d_probs = jnp.einsum("qhd,khd->hqk", do_h, vc_h, preferred_element_type=F32)
    inner = jnp.sum(probs * d_probs, axis=-1, keepdims=True)
    d_scores = (probs * (d_probs - inner)).astype(BF)
    d_vc = seq_sum(jnp.einsum("hqk,qhd->khd", p_low, do_h, preferred_element_type=F32))
    d_vc = d_vc.reshape(-1, width).astype(BF)
    d_kc = seq_sum(jnp.einsum("hqk,qhd->khd", d_scores, q_h, preferred_element_type=F32) * scale)
    d_kc = d_kc.reshape(-1, width).astype(BF)
    d_query = jnp.einsum("hqk,khd->qhd", d_scores, kc_h, preferred_element_type=F32) * scale
    d_query = d_query.reshape(mine, width).astype(BF)
    d_key = t_mm(e_mask, d_kc).astype(BF)
    d_value = t_mm(e_mask, d_vc).astype(BF)
    d_e = jnp.where(valid[:, None], mm_t(key, d_kc) + mm_t(value, d_vc), 0.0)
    attn = []
    for split, whole in ((h, d_query), (h, d_key), (h, d_value), (attended, d_attn)):
        g = pair_grad(split, whole)
        attn.append(reduce_grad(grid, g.reshape(ny, nx, width // n_rows, n_kc, width // n_kc)))
    d_h = mm_t(d_query, w_query) + mm_t(d_key, w_key) + mm_t(d_value, w_value)
    gg_attn = jnp.sum(d_h * n1, axis=0)
    grad_in = spread_seq((d_mid + norm_back(n1, r1, gain_attn, d_h)).astype(BF))

    if share > 1:
        d_e = lax.dynamic_update_slice(
            jnp.zeros((seq_len, d_e.shape[1]), F32), d_e, (my_part * mine, 0)
        )
    e_rows, e_cols = seq_len // n_rows, d_e.shape[1] // n_kc
    d_e = d_e.reshape(n_rows, e_rows, n_kc, e_cols).transpose(0, 2, 1, 3)
    g_cols = width // n_rows
    gains = jnp.stack([gg_attn, gg_ffn]).reshape(2, n_rows, g_cols).transpose(1, 0, 2)
    gains = jnp.broadcast_to(gains[:, None], (n_rows, n_kc, 2, g_cols))
    small = jnp.concatenate(
        [d_e.reshape(n_rows, n_kc, -1), gains.reshape(n_rows, n_kc, -1)], axis=2
    )
    small = small.reshape(ny, nx, nc, n_kc, -1)
    if nc > 1:
        small = grid.scatter_sum(small, 2, "c")
    small = grid.scatter_sum(small, 1, "x")
    small = grid.scatter_sum(small, 0, "y")
    small = grid.scatter_sum(small, 0, "z")
    n_e = e_rows * e_cols
    return (
        output,
        grad_in,
        attn[0],
        attn[1],
        attn[2],
        attn[3],
        g_up,
        g_down,
        small[n_e : n_e + g_cols],
        small[n_e + g_cols :],
        small[:n_e].reshape(e_rows, e_cols),
    )


def solution(mesh):
    tokens = P(None, ("rows", "kc"), None)
    return jax.shard_map(
        local,
        mesh=mesh,
        in_specs=(tokens,) + (P(),) * 8 + (P(None, "kc"), P(None, "rows"), tokens),
        out_specs=(tokens, tokens) + (P("rows", "kc"),) * 6 + (P("rows"), P("rows"))
        + (P("rows", "kc"),),
        check_vma=False,
    )
```

```python
import functools
import math

import jax
import jax.numpy as jnp
from jax import lax
from jax.experimental import pallas as pl
from jax.experimental.pallas import tpu as pltpu
from jax.sharding import PartitionSpec as P

HEAD = 64
BF = jnp.bfloat16
F32 = jnp.float32


def normed(values):
    centred = values - jnp.mean(values, axis=-1, keepdims=True)
    rstd = lax.rsqrt(jnp.mean(centred * centred, axis=-1, keepdims=True) + 1e-05)
    return centred * rstd, rstd


def norm_back(n, rstd, gain, d):
    dc = d * gain
    return rstd * (
        dc - jnp.mean(dc, axis=-1, keepdims=True) - n * jnp.mean(dc * n, axis=-1, keepdims=True)
    )


def mm(left, right):
    return jnp.dot(left, right, preferred_element_type=F32)


def mm_t(left, right):
    return jnp.einsum("ta,ba->tb", left, right, preferred_element_type=F32)


def t_mm(left, right):
    return jnp.einsum("ta,tb->ab", left, right, preferred_element_type=F32)


class Grid:
    def __init__(self, n_rows, n_kc):
        self.n_rows, self.n_kc = n_rows, n_kc
        self.nc = 2 if n_rows % 2 == 0 else 1
        plane = n_rows // self.nc
        self.nx = next(d for d in range(math.isqrt(plane), 0, -1) if plane % d == 0)
        self.ny = plane // self.nx
        row = lax.axis_index("rows")
        self.c = row % self.nc
        self.x = (row // self.nc) % self.nx
        self.y = row // (self.nc * self.nx)
        self.z = lax.axis_index("kc")

    def send(self, value, axis, shift):
        if axis == "z":
            n = self.n_kc
            return lax.ppermute(value, "kc", [(i, (i + shift) % n) for i in range(n)])
        pairs = []
        for i in range(self.n_rows):
            c, x, y = i % self.nc, (i // self.nc) % self.nx, i // (self.nc * self.nx)
            if axis == "c":
                c = (c + shift) % self.nc
            elif axis == "x":
                x = (x + shift) % self.nx
            else:
                y = (y + shift) % self.ny
            pairs.append((i, (y * self.nx + x) * self.nc + c))
        return lax.ppermute(value, "rows", pairs)

    def scatter_sum(self, value, dim, axis):
        n = {"c": self.nc, "x": self.nx, "y": self.ny, "z": self.n_kc}[axis]
        me = {"c": self.c, "x": self.x, "y": self.y, "z": self.z}[axis]
        total = lax.dynamic_index_in_dim(value, me, dim, keepdims=False).astype(F32)
        for shift in range(1, n):
            block = lax.dynamic_index_in_dim(value, (me + shift) % n, dim, keepdims=False)
            total = total + self.send(block, axis, shift).astype(F32)
        return total


def reduce_grad(grid, value, low=True):
    kind = BF if low else F32
    half = value.shape[2] // 2
    if half % 16:
        parts = ((value, "x"),)
    else:
        parts = ((value[:, :, :half], "x"), (value[:, :, half:], "y"))
    done = []
    for part, first in parts:
        part = part.astype(kind)
        if first == "x":
            part = grid.scatter_sum(part, 1, "x").astype(kind)
            part = grid.scatter_sum(part, 0, "y").astype(kind)
        else:
            part = grid.scatter_sum(part, 0, "y").astype(kind)
            part = grid.scatter_sum(part, 0, "x").astype(kind)
        done.append(grid.scatter_sum(part, 1, "z"))
    return jnp.concatenate(done, axis=0)


def general(
    inputs,
    w_query,
    w_key,
    w_value,
    w_out,
    w_up,
    w_down,
    gain_attn,
    gain_ffn,
    proj_e,
    lengths,
    cotangent,
):
    batches, t, width = inputs.shape
    heads = width // HEAD
    ff = w_up.shape[1]
    scale = HEAD ** (-0.5)
    n_rows, n_kc = lax.axis_size("rows"), lax.axis_size("kc")
    grid = Grid(n_rows, n_kc)
    share = n_kc // batches
    seq_len = proj_e.shape[0]
    mine = batches * t
    my_batch, my_part = grid.z // share, grid.z % share
    lane, part = grid.z % batches, grid.z // batches

    def reorder(got, first):
        stacked = jnp.stack(got)
        return jnp.stack(
            [
                lax.dynamic_index_in_dim(stacked, (first - i) % batches, 0, keepdims=False)
                for i in range(batches)
            ]
        )

    def gather_seq(v):
        got = []
        for j in range(batches):
            block = lax.dynamic_index_in_dim(v, (lane + j) % batches, 0, keepdims=False)
            pairs = [
                (i, ((i % batches + j) % batches) * share + i // batches) for i in range(n_kc)
            ]
            got.append(block if all(a == b for a, b in pairs) else lax.ppermute(block, "kc", pairs))
        return reorder(got, my_batch).reshape(mine, width)

    def spread_seq(v):
        blocks = v.reshape(batches, t, width)
        got = []
        for j in range(batches):
            block = lax.dynamic_index_in_dim(blocks, (my_batch - j) % batches, 0, keepdims=False)
            pairs = [
                (((i % batches + j) % batches) * share + i // batches, i) for i in range(n_kc)
            ]
            got.append(block if all(a == b for a, b in pairs) else lax.ppermute(block, "kc", pairs))
        return reorder(got[:1] + got[:0:-1], lane + batches).reshape(inputs.shape)

    def seq_sum(v):
        if share == 1:
            return v
        groups = [[b * share + p for p in range(share)] for b in range(batches)]
        return lax.psum(v, "kc", axis_index_groups=groups)

    x_low = gather_seq(inputs)
    e_t = lax.all_gather(proj_e.T, "kc", axis=0, tiled=True)
    dy = gather_seq(cotangent)
    e_t = lax.dynamic_slice_in_dim(e_t, my_part * mine, mine, 1)
    length = lax.dynamic_index_in_dim(lengths, my_batch, 0, keepdims=False)[0]
    valid = (my_part * mine + jnp.arange(mine)) < length
    e_mask = jnp.where(valid[None, :], e_t, jnp.zeros_like(e_t))

    x = x_low.astype(F32)
    n1, r1 = normed(x)
    h = (n1 * gain_attn).astype(BF)
    query, key, value = (mm(h, w).astype(BF) for w in (w_query, w_key, w_value))
    k_comp = seq_sum(mm(e_mask, key)).astype(BF)
    v_comp = seq_sum(mm(e_mask, value)).astype(BF)
    q_h = query.reshape(mine, heads, HEAD)
    kc_h = k_comp.reshape(-1, heads, HEAD)
    vc_h = v_comp.reshape(-1, heads, HEAD)
    scores = jnp.einsum("qhd,khd->hqk", q_h, kc_h, preferred_element_type=F32) * scale
    probs = jax.nn.softmax(scores, axis=-1)
    p_low = probs.astype(BF)
    attended = (
        jnp.einsum("hqk,khd->qhd", p_low, vc_h, preferred_element_type=F32)
        .reshape(mine, width)
        .astype(BF)
    )
    mid = x + mm(attended, w_out)
    n2, r2 = normed(mid)
    h2 = (n2 * gain_ffn).astype(BF)
    up = mm(h2, w_up)
    act = jax.nn.gelu(up).astype(BF)
    output = spread_seq((mid + mm(act, w_down)).astype(BF))

    nc, nx, ny = grid.nc, grid.nx, grid.ny

    def by_core(v):
        v = v.reshape(mine, ny * nx, nc, -1)
        own = lax.dynamic_index_in_dim(v, grid.c, 2, keepdims=False)
        other = lax.dynamic_index_in_dim(v, nc - 1 - grid.c, 2, keepdims=False)
        return own.reshape(mine, -1), other.reshape(mine, -1)

    def pair_grad(split, whole):
        own, other = by_core(split)
        return t_mm(own, whole) + t_mm(grid.send(other, "c", 1), grid.send(whole, "c", 1))

    g_down = pair_grad(act, dy)
    g_down = reduce_grad(grid, g_down.reshape(ny, nx, ff // n_rows, n_kc, width // n_kc))
    d_act = mm_t(dy, w_down)
    d_up = jax.vjp(jax.nn.gelu, up)[1](d_act)[0].astype(BF)
    g_up = pair_grad(h2, d_up)
    g_up = reduce_grad(grid, g_up.reshape(ny, nx, width // n_rows, n_kc, ff // n_kc))
    d_h2 = mm_t(d_up, w_up)
    gg_ffn = jnp.sum(d_h2 * n2, axis=0)
    d_mid = dy.astype(F32) + norm_back(n2, r2, gain_ffn, d_h2)
    d_attn = d_mid.astype(BF)
    d_att = mm_t(d_attn, w_out).astype(BF)
    do_h = d_att.reshape(mine, heads, HEAD)
    d_probs = jnp.einsum("qhd,khd->hqk", do_h, vc_h, preferred_element_type=F32)
    inner = jnp.sum(probs * d_probs, axis=-1, keepdims=True)
    d_scores = (probs * (d_probs - inner)).astype(BF)
    d_vc = seq_sum(jnp.einsum("hqk,qhd->khd", p_low, do_h, preferred_element_type=F32))
    d_vc = d_vc.reshape(-1, width).astype(BF)
    d_kc = seq_sum(jnp.einsum("hqk,qhd->khd", d_scores, q_h, preferred_element_type=F32) * scale)
    d_kc = d_kc.reshape(-1, width).astype(BF)
    d_query = jnp.einsum("hqk,khd->qhd", d_scores, kc_h, preferred_element_type=F32) * scale
    d_query = d_query.reshape(mine, width).astype(BF)
    d_key = t_mm(e_mask, d_kc).astype(BF)
    d_value = t_mm(e_mask, d_vc).astype(BF)
    d_e = jnp.where(valid[:, None], mm_t(key, d_kc) + mm_t(value, d_vc), 0.0)
    attn = []
    for split, whole in ((h, d_query), (h, d_key), (h, d_value), (attended, d_attn)):
        g = pair_grad(split, whole)
        attn.append(reduce_grad(grid, g.reshape(ny, nx, width // n_rows, n_kc, width // n_kc)))
    d_h = mm_t(d_query, w_query) + mm_t(d_key, w_key) + mm_t(d_value, w_value)
    gg_attn = jnp.sum(d_h * n1, axis=0)
    grad_in = spread_seq((d_mid + norm_back(n1, r1, gain_attn, d_h)).astype(BF))

    if share > 1:
        d_e = lax.dynamic_update_slice(
            jnp.zeros((seq_len, d_e.shape[1]), F32), d_e, (my_part * mine, 0)
        )
    small = small_sum(grid, d_e, jnp.stack([gg_attn, gg_ffn]))
    return (output, grad_in, *attn, g_up, g_down, *small)


VMEM_LIMIT = 48 * 1024 * 1024
MANY = pl.BlockSpec(memory_space=pl.ANY)
SCALARS = pl.BlockSpec(memory_space=pltpu.SMEM)
VM = pl.BlockSpec(memory_space=pltpu.VMEM)


def here():
    row = lax.axis_index("rows")
    return row & 1, row >> 1, lax.axis_index("kc")


def nt(left, right):
    return lax.dot_general(left, right, (((1,), (1,)), ((), ())), preferred_element_type=F32)


def sds(*shape, dtype=BF):
    return jax.ShapeDtypeStruct(shape, dtype)


def call(body, outs, args, specs=None, scratch=(), out_specs=None, cost=None):
    return pl.pallas_call(
        body,
        out_shape=outs,
        in_specs=specs or [VM] * len(args),
        out_specs=out_specs or [VM] * len(outs),
        scratch_shapes=list(scratch),
        compiler_params=pltpu.CompilerParams(vmem_limit_bytes=VMEM_LIMIT),
        cost_estimate=pl.CostEstimate(
            flops=cost or 1000, bytes_accessed=1000000, transcendentals=0
        ),
    )(*args)


def transposed(value):
    return jnp.transpose(value.astype(F32)).astype(BF)


def pack_kernel(n, x_ref, e_ref, c_ref, *outs):
    _, _, z = here()
    width = x_ref.shape[2]
    e_t = transposed(e_ref[...])
    for j in range(n):
        outs[j][:, :width] = x_ref[(z + j) & (n - 1)]
        outs[j][:, width:] = e_t
        outs[n + j][...] = c_ref[(z + j) & (n - 1)]


def gelu_both(u):
    s = math.sqrt(2.0 / math.pi)
    u2 = u * u
    th = jnp.tanh(u * (s + (s * 0.044715) * u2))
    half = 0.5 * (1.0 + th)
    slope = half + (0.5 * u) * (1.0 - th * th) * (s + (3.0 * s * 0.044715) * u2)
    return u * half, slope


def halves(value):
    low = lax.broadcasted_iota(jnp.int32, value.shape, 1) < HEAD
    zero = jnp.zeros_like(value)
    return jnp.where(low, value, zero), jnp.where(low, zero, value)


def softmax_rows(scores):
    expo = jnp.exp(scores - jnp.max(scores, axis=0, keepdims=True))
    return expo / jnp.sum(expo, axis=0, keepdims=True)


def forward_kernel(n, *refs):
    xe = refs[:n]
    len_ref, ga_ref, gf_ref = refs[n : n + 3]
    w_hbm = refs[n + 3 : n + 8]
    outs = refs[n + 8 : n + 21]
    w_vm = refs[n + 21 : n + 26]
    act_s, lt_s, gp_s, q_s, k_s, v_s, kc_s, vc_s, mid_s, x_s, em_s, et_s, att_t = refs[
        n + 26 : n + 39
    ]
    w_sem, o_sem = refs[n + 39 :]
    loads = [
        pltpu.make_async_copy(a, b, w_sem.at[i]) for i, (a, b) in enumerate(zip(w_hbm, w_vm))
    ]
    for load in loads:
        load.start()
    core, xy, z = here()
    t, wide = xe[0].shape
    mine = t * n
    width = x_s.shape[1]
    ff = w_vm[4].shape[1]
    stores = []

    def store(src, i):
        stores.append(pltpu.make_async_copy(src, outs[i], o_sem.at[i]))
        stores[-1].start()

    def rows_by_core(i, value):
        value_t = jnp.transpose(value).astype(BF)
        part = width // 8
        for b in range(4):
            for a in range(2):
                first = (2 * b + a) * part
                lt_s[a ^ core, i, b ^ xy] = value_t[first : first + part]

    for j in range(n):
        at = pl.multiple_of(((z - j) & (n - 1)) * t, t)
        x_s[pl.ds(at, t), :] = xe[j][:, :width]
        et_s[pl.ds(at, t), :] = xe[j][:, width:]
    store(x_s, 11)
    x = x_s[...].astype(F32)
    n1, _ = normed(x)
    h = n1 * ga_ref[...]
    rows_by_core(0, h)
    h = h.astype(BF)
    keep = lax.broadcasted_iota(jnp.int32, et_s.shape, 1) < len_ref[z, 0]
    e_t = jnp.where(keep, et_s[...].astype(F32), 0.0)
    em_s[...] = jnp.transpose(e_t).astype(BF)
    store(em_s, 12)
    e_t = e_t.astype(BF)
    loads[0].wait()
    q_s[...] = mm(h, w_vm[0][...]).astype(BF)
    store(q_s, 5)
    loads[1].wait()
    k_s[...] = mm(h, w_vm[1][...]).astype(BF)
    store(k_s, 6)
    loads[2].wait()
    v_s[...] = mm(h, w_vm[2][...]).astype(BF)
    store(v_s, 7)
    kc_s[...] = mm(e_t, k_s[...]).astype(BF)
    store(kc_s, 8)
    v_comp = mm(e_t, v_s[...])
    vc_s[...] = v_comp.astype(BF)
    store(vc_s, 9)
    vc_t = jnp.transpose(v_comp).astype(BF)
    for p in range(width // 128):
        lanes = slice(128 * p, 128 * p + 128)
        q2 = q_s[:, lanes]
        for i, kc in enumerate(halves(kc_s[:, lanes])):
            probs = softmax_rows(nt(kc, q2) * HEAD ** (-0.5)).astype(BF)
            first = 128 * p + HEAD * i
            att_t[first : first + HEAD, :] = mm(vc_t[first : first + HEAD, :], probs)
    att = jnp.transpose(att_t[...])
    rows_by_core_t = att_t[...].astype(BF)
    part = width // 8
    for b in range(4):
        for a in range(2):
            first = (2 * b + a) * part
            lt_s[a ^ core, 1, b ^ xy] = rows_by_core_t[first : first + part]
    loads[3].wait()
    mid = x + mm(att.astype(BF), w_vm[3][...])
    mid_s[...] = mid
    store(mid_s, 10)
    n2, _ = normed(mid)
    h2 = n2 * gf_ref[...]
    rows_by_core(2, h2)
    store(lt_s.at[0], 2)
    store(lt_s.at[1], 3)
    h2 = h2.astype(BF)
    loads[4].wait()
    step = ff // 4
    for b in range(4):
        act, slope = gelu_both(mm(h2, w_vm[4][:, b * step : (b + 1) * step]))
        gp_s[:, b * step : (b + 1) * step] = slope.astype(BF)
        act = act.astype(BF)
        for a in range(2):
            act_s[a ^ core, b ^ xy] = act[:, a * (step // 2) : (a + 1) * (step // 2)]
    store(act_s.at[0], 0)
    store(act_s.at[1], 1)
    store(gp_s, 4)
    for copy in stores:
        copy.wait()


def gather_dy_kernel(n, *refs):
    blocks, (dy_ref, dyt_ref), dy_s = refs[:n], refs[n : n + 2], refs[n + 2]
    _, _, z = here()
    t, width = blocks[0].shape
    for j in range(n):
        at = pl.multiple_of(((z - j) & (n - 1)) * t, t)
        dy_s[pl.ds(at, t), :] = blocks[j][...]
    dy = dy_s[...]
    dy_ref[...] = dy
    dy_t = transposed(dy)
    part = width // n
    for b in range(n):
        dyt_ref[b ^ z] = dy_t[b * part : (b + 1) * part]


def d_up_kernel(dy_ref, gp_ref, wd_hbm, out_ref, wd_s, sem):
    n = out_ref.shape[0]
    step = wd_s.shape[1]
    loads = [
        pltpu.make_async_copy(wd_hbm.at[pl.ds(b * step, step)], wd_s.at[b], sem.at[b])
        for b in range(n)
    ]
    for load in loads:
        load.start()
    _, _, z = here()
    dy = dy_ref[...]
    for b in range(n):
        loads[b].wait()
        d_act = nt(dy, wd_s[b])
        slope = gp_ref[:, b * step : (b + 1) * step].astype(F32)
        out_ref[b ^ z] = (slope * d_act).astype(BF)


def scatter_blocks(outs, r, k, low, high):
    keep_a, send_a, keep_b, send_b = outs
    r_y, r_x = r >> 1, r & 1
    (send_a if r_x else keep_a)[r_y, k] = low
    (send_b if r_y else keep_b)[r_x, k] = high


def grad_down_kernel(lo_ref, lr_ref, ro_ref, rr_ref, *outs):
    n, part, tokens = lo_ref.shape
    lo = lo_ref[...].reshape(n * part, tokens)
    lr = lr_ref[...].reshape(n * part, tokens)
    for r in range(4):
        g = (mm(lo, ro_ref[r]) + mm(lr, rr_ref[r])).astype(BF)
        for k in range(n):
            low = g[k * part : k * part + part // 2]
            scatter_blocks(outs, r, k, low, g[k * part + part // 2 : (k + 1) * part])


def grad_up_kernel(lo_ref, lr_ref, ro_ref, rr_ref, *outs):
    _, part, tokens = lo_ref.shape[1:]
    lo = lo_ref[2].reshape(4 * part, tokens)
    lr = lr_ref[2].reshape(4 * part, tokens)
    for k in range(ro_ref.shape[0]):
        g = (mm(lo, ro_ref[k]) + mm(lr, rr_ref[k])).astype(BF)
        for r in range(4):
            low = g[r * part : r * part + part // 2]
            scatter_blocks(outs, r, k, low, g[r * part + part // 2 : (r + 1) * part])


def grad_attn_kernel(lo_ref, lr_ref, ro_ref, rr_ref, *outs):
    _, part, tokens = lo_ref.shape[1:]
    left = [ref[i].reshape(4 * part, tokens) for i in range(2) for ref in (lo_ref, lr_ref)]
    width = ro_ref.shape[2]
    cut = (width * 3 // 4) // 256 * 256
    rest = width * 3 // 4 - cut
    for k in range(ro_ref.shape[0]):
        tail = []
        for ref in (ro_ref, rr_ref):
            v = ref[k, :, cut:]
            first = lax.broadcasted_iota(jnp.int32, v.shape, 1) < rest
            tail.append((jnp.where(first, v, 0), jnp.where(first, 0, v)))
        head = mm(left[0], ro_ref[k, :, :cut]) + mm(left[1], rr_ref[k, :, :cut])
        mixed = (mm(left[0], tail[0][0]) + mm(left[1], tail[1][0])) + (
            mm(left[2], tail[0][1]) + mm(left[3], tail[1][1])
        )
        g = jnp.concatenate([head, mixed], axis=1).astype(BF)
        for r in range(4):
            low = g[r * part : r * part + part // 2]
            scatter_blocks(outs, r, k, low, g[r * part + part // 2 : (r + 1) * part])


def first_sum_kernel(ka, ra, kb, rb, oa, ob):
    oa[...] = (ka[1].astype(F32) + ra[1].astype(F32)).astype(BF)
    ob[...] = (kb[1].astype(F32) + rb[1].astype(F32)).astype(BF)


def second_sum_kernel(ka, ra, ra2, kb, rb, rb2, keep, send):
    for i, (k_ref, r_ref, r2_ref) in enumerate(((ka, ra, ra2), (kb, rb, rb2))):
        for k in range(4):
            total = (k_ref[0, k].astype(F32) + r_ref[0, k].astype(F32)) + r2_ref[k].astype(F32)
            (send if k & 1 else keep)[k >> 1, i] = total.astype(BF)


def third_sum_kernel(keep, got, out):
    out[...] = (keep[1].astype(F32) + got[1].astype(F32)).astype(BF)


def total_of(keep, got, last, i):
    return (keep[0, i].astype(F32) + got[0, i].astype(F32)) + last[i].astype(F32)


def last_rows_kernel(keep, got, last, out):
    half = keep.shape[2]
    for i in range(2):
        out[i * half : (i + 1) * half] = total_of(keep, got, last, i)


def last_turned_kernel(keep, got, last, out):
    out[...] = jnp.transpose(
        jnp.concatenate([total_of(keep, got, last, i) for i in range(2)], axis=0)
    )


def last_split_kernel(keep, got, last, *outs):
    half = keep.shape[2]
    for i in range(2):
        total = total_of(keep, got, last, i)
        part = total.shape[1] // len(outs)
        for j, out in enumerate(outs):
            out[i * half : (i + 1) * half] = total[:, j * part : (j + 1) * part]


def backward_kernel(
    du_ref, dy_ref, mid_ref, gf_ref, q_ref, k_ref, v_ref, kc_ref, vc_ref, em_ref, len_ref,
    wu_hbm, wo_hbm,
    r_ref, dq_ref, dk_ref, dv_ref, dmid_ref, ggf_ref, gpe_ref,
    wu_s, wo_s, dkc_s, dvc_s, dqt_s, sem,
):
    loads = [
        pltpu.make_async_copy(wu_hbm, wu_s, sem.at[0]),
        pltpu.make_async_copy(wo_hbm, wo_s, sem.at[1]),
    ]
    for load in loads:
        load.start()
    _, _, z = here()
    n = du_ref.shape[0]
    width = dy_ref.shape[1]
    step = wu_s.shape[1] // n
    mid = mid_ref[...]
    n2, r2 = normed(mid)
    loads[0].wait()
    d_h2 = nt(du_ref[z], wu_s[:, :step])
    for b in range(1, n):
        d_h2 = d_h2 + nt(du_ref[b ^ z], wu_s[:, b * step : (b + 1) * step])
    ggf_ref[...] = jnp.sum(d_h2 * n2, axis=0, keepdims=True)
    d_mid = dy_ref[...].astype(F32) + norm_back(n2, r2, gf_ref[...], d_h2)
    dmid_ref[...] = d_mid
    d_attn = d_mid.astype(BF)
    loads[1].wait()
    d_att = nt(d_attn, wo_s[...]).astype(BF)
    scale = HEAD ** (-0.5)
    kc_t = transposed(kc_ref[...])
    for p in range(width // 128):
        lanes = slice(128 * p, 128 * p + 128)
        q2, do2 = q_ref[:, lanes], d_att[:, lanes]
        q_pair, do_pair = halves(q2), halves(do2)
        kc_pair, vc_pair = halves(kc_ref[:, lanes]), halves(vc_ref[:, lanes])
        dvc, dkc = 0.0, 0.0
        for i in range(2):
            probs = softmax_rows(nt(kc_pair[i], q2) * scale)
            d_probs = nt(vc_pair[i], do2)
            inner = jnp.sum(probs * d_probs, axis=0, keepdims=True)
            d_scores = (probs * (d_probs - inner)).astype(BF)
            dvc = dvc + mm(probs.astype(BF), do_pair[i])
            dkc = dkc + mm(d_scores, q_pair[i])
            first = 128 * p + HEAD * i
            dqt_s[first : first + HEAD, :] = mm(kc_t[first : first + HEAD, :], d_scores)
        dvc_s[:, lanes] = dvc.astype(BF)
        dkc_s[:, lanes] = (dkc * scale).astype(BF)
    em = em_ref[...]
    dkc, dvc = dkc_s[...], dvc_s[...]
    d_query = jnp.transpose(dqt_s[...] * scale)
    d_key, d_value = mm(em, dkc), mm(em, dvc)
    keep = lax.broadcasted_iota(jnp.int32, gpe_ref.shape, 0) < len_ref[z, 0]
    gpe_ref[...] = jnp.where(keep, nt(k_ref[...], dkc) + nt(v_ref[...], dvc), 0.0)
    part = width // n
    for i, value in enumerate((d_query, d_key, d_value, d_mid)):
        for b in range(n):
            r_ref[b ^ z, :, i * part : (i + 1) * part] = value[:, b * part : (b + 1) * part].astype(BF)
    dq_ref[...] = d_query.astype(BF)
    dk_ref[...] = d_key.astype(BF)
    dv_ref[...] = d_value.astype(BF)


def output_kernel(
    n, dq_ref, dk_ref, dv_ref, x_ref, ga_ref, dmid_ref, mid_ref, ao_ref, ar_ref,
    wq_ref, wk_ref, wv_ref, wd_ref, *refs,
):
    outs, gga_ref, out_s, gi_s = refs[:n], refs[n], refs[n + 1], refs[n + 2]
    core, xy, z = here()
    d_h = nt(dq_ref[...], wq_ref[...]) + nt(dk_ref[...], wk_ref[...]) + nt(dv_ref[...], wv_ref[...])
    n1, r1 = normed(x_ref[...].astype(F32))
    gga_ref[...] = jnp.sum(d_h * n1, axis=0, keepdims=True)
    gi_s[...] = (dmid_ref[...] + norm_back(n1, r1, ga_ref[...], d_h)).astype(BF)
    total = mid_ref[...]
    part = ao_ref.shape[2]
    for r in range(4):
        for a, ref in enumerate((ao_ref, ar_ref)):
            first = pl.multiple_of(((r ^ xy) * 2 + (a ^ core)) * part, part)
            total = total + mm(ref[r], wd_ref[pl.ds(first, part), :])
    out_s[...] = total.astype(BF)
    t = outs[0].shape[1]
    for j in range(n):
        at = pl.multiple_of(((z - j) & (n - 1)) * t, t)
        outs[j][0] = out_s[pl.ds(at, t), :]
        outs[j][1] = gi_s[pl.ds(at, t), :]


def unpack_kernel(n, *refs):
    _, _, z = here()
    for j in range(n):
        refs[n][(z + j) & (n - 1)] = refs[j][0]
        refs[n + 1][(z + j) & (n - 1)] = refs[j][1]


def fast(
    inputs, w_query, w_key, w_value, w_out, w_up, w_down, gain_attn, gain_ffn, proj_e, lengths,
    cotangent,
):
    n, t, width = inputs.shape
    ff = w_up.shape[1]
    k_block = proj_e.shape[1]
    mine, k_dim = n * t, n * k_block
    wide = width + mine
    grid = Grid(lax.axis_size("rows"), n)
    ga, gf = gain_attn[None], gain_ffn[None]

    packed = call(
        functools.partial(pack_kernel, n),
        [sds(t, wide)] * n + [sds(t, width)] * n,
        (inputs, proj_e, cotangent),
    )
    xe = [packed[0]] + [grid.send(packed[j], "z", j) for j in range(1, n)]
    dyb = [packed[n]] + [grid.send(packed[n + j], "z", j) for j in range(1, n)]

    square = (mine, width)
    sixth = width // 8
    out = [
        sds(4, mine, ff // 8), sds(4, mine, ff // 8),
        sds(3, 4, sixth, mine), sds(3, 4, sixth, mine),
        sds(mine, ff), sds(*square), sds(*square), sds(*square),
        sds(k_dim, width), sds(k_dim, width), sds(*square, dtype=F32), sds(*square),
        sds(mine, k_dim),
    ]
    weights = (w_query, w_key, w_value, w_out, w_up)
    scratch = [pltpu.VMEM(w.shape, BF) for w in weights] + [
        pltpu.VMEM((2, 4, mine, ff // 8), BF),
        pltpu.VMEM((2, 3, 4, sixth, mine), BF),
    ]
    scratch += [pltpu.VMEM(o.shape, o.dtype) for o in out[4:]]
    scratch += [
        pltpu.VMEM((k_dim, mine), BF),
        pltpu.VMEM((width, mine), F32),
        pltpu.SemaphoreType.DMA((len(weights),)),
        pltpu.SemaphoreType.DMA((len(out),)),
    ]
    act_own, act_oth, lt_own, lt_oth, gp, q, k, v, kc, vc, mid, x_nat, em = call(
        functools.partial(forward_kernel, n),
        out,
        (*xe, lengths, ga, gf, *weights),
        [VM] * n + [SCALARS, VM, VM] + [MANY] * 5,
        scratch,
        [MANY] * len(out),
        cost=4_000_000_000,
    )
    act_got = grid.send(act_oth, "c", 1)
    dy, dyt = call(
        functools.partial(gather_dy_kernel, n),
        [sds(*square), sds(n, width // n, mine)],
        dyb,
        scratch=[pltpu.VMEM(square, BF)],
    )
    dyt_got = grid.send(dyt, "c", 1)
    lt_got = grid.send(lt_oth, "c", 1)
    du = call(
        d_up_kernel,
        [sds(n, mine, ff // n)],
        (dy, gp, w_down),
        [VM, VM, MANY],
        [pltpu.VMEM((n, ff // n, width), BF), pltpu.SemaphoreType.DMA((n,))],
        cost=1_300_000_000,
    )[0]
    du_got = grid.send(du, "c", 1)

    def scatter(parts):
        keep_a, send_a, keep_b, send_b = parts
        got_a, got_b = grid.send(send_a, "x", 1), grid.send(send_b, "y", 1)
        shape = keep_a.shape
        next_a, next_b = call(
            first_sum_kernel, [sds(*shape[1:])] * 2, (keep_a, got_a, keep_b, got_b)
        )
        got_a2, got_b2 = grid.send(next_a, "y", 1), grid.send(next_b, "x", 1)
        keep, send = call(
            second_sum_kernel,
            [sds(2, 2, *shape[2:])] * 2,
            (keep_a, got_a, got_a2, keep_b, got_b, got_b2),
        )
        got = lax.ppermute(send, "kc", [(i, i ^ 1) for i in range(n)])
        third = call(third_sum_kernel, [sds(2, *shape[2:])], (keep, got))[0]
        last = lax.ppermute(third, "kc", [(i, i ^ 2) for i in range(n)])
        return keep, got, last

    down_parts = [sds(2, n, width // n // 2, ff // 8)] * 4
    g_down = scatter(
        call(grad_down_kernel, down_parts, (dyt, dyt_got, act_own, act_got), cost=1_300_000_000)
    )
    up_parts = [sds(2, n, sixth // 2, ff // n)] * 4
    g_up = scatter(
        call(grad_up_kernel, up_parts, (lt_own, lt_got, du, du_got), cost=1_300_000_000)
    )
    r_own, dq, dk, dv, d_mid, ggf, gpe = call(
        backward_kernel,
        [
            sds(n, mine, width), sds(*square), sds(*square), sds(*square),
            sds(*square, dtype=F32), sds(1, width, dtype=F32), sds(mine, k_dim, dtype=F32),
        ],
        (du, dy, mid, gf, q, k, v, kc, vc, em, lengths, w_up, w_out),
        [VM] * 10 + [SCALARS, MANY, MANY],
        [
            pltpu.VMEM(w_up.shape, BF), pltpu.VMEM(w_out.shape, BF),
            pltpu.VMEM((k_dim, width), BF), pltpu.VMEM((k_dim, width), BF),
            pltpu.VMEM((width, mine), F32), pltpu.SemaphoreType.DMA((2,)),
        ],
        cost=4_000_000_000,
    )
    r_got = grid.send(r_own, "c", 1)
    attn_parts = [sds(2, n, sixth // 2, width)] * 4
    g_attn = scatter(
        call(grad_attn_kernel, attn_parts, (lt_own, lt_got, r_own, r_got), cost=1_600_000_000)
    )
    blocks = call(
        functools.partial(output_kernel, n),
        [sds(2, t, width)] * n + [sds(1, width, dtype=F32)],
        (dq, dk, dv, x_nat, ga, d_mid, mid, act_own, act_oth, w_query, w_key, w_value, w_down),
        scratch=[pltpu.VMEM(square, BF), pltpu.VMEM(square, BF)],
        cost=2_500_000_000,
    )
    gga = blocks[n]
    back = [blocks[0]] + [grid.send(blocks[j], "z", n - j) for j in range(1, n)]
    output, grad_in = call(
        functools.partial(unpack_kernel, n), [sds(*inputs.shape)] * 2, back
    )
    small = small_sum(grid, gpe, jnp.concatenate([gga, ggf], axis=0))
    (g_up,) = call(last_rows_kernel, [sds(sixth, ff // n, dtype=F32)], g_up)
    (g_down,) = call(last_turned_kernel, [sds(ff // 8, width // n, dtype=F32)], g_down)
    attn = call(last_split_kernel, [sds(sixth, width // n, dtype=F32)] * 4, g_attn)
    return (output, grad_in, *attn, g_up, g_down, *small)


def small_sum(grid, d_e, gains):
    n_rows, n_kc = grid.n_rows, grid.n_kc
    e_rows, e_cols = d_e.shape[0] // n_rows, d_e.shape[1] // n_kc
    d_e = d_e.reshape(n_rows, e_rows, n_kc, e_cols).transpose(0, 2, 1, 3)
    g_cols = gains.shape[1] // n_rows
    gains = gains.reshape(2, n_rows, g_cols).transpose(1, 0, 2)
    gains = jnp.broadcast_to(gains[:, None], (n_rows, n_kc, 2, g_cols))
    small = jnp.concatenate(
        [d_e.reshape(n_rows, n_kc, -1), gains.reshape(n_rows, n_kc, -1)], axis=2
    )
    small = small.reshape(grid.ny, grid.nx, grid.nc, n_kc, -1)
    if grid.nc > 1:
        small = grid.scatter_sum(small, 2, "c")
    small = grid.scatter_sum(small, 1, "x")
    small = grid.scatter_sum(small, 0, "y")
    small = grid.scatter_sum(small, 0, "z")
    n_e = e_rows * e_cols
    return (
        small[n_e : n_e + g_cols],
        small[n_e + g_cols :],
        small[:n_e].reshape(e_rows, e_cols),
    )


def local(*args):
    inputs, w_up, proj_e = args[0], args[5], args[9]
    n, t, width = inputs.shape
    mine = n * t
    fits = (
        lax.axis_size("rows") == 8
        and lax.axis_size("kc") == n == 4
        and proj_e.shape == (mine, t)
        and mine % 128 == 0
        and width % 768 == 0
        and w_up.shape[1] == 4 * width
    )
    return fast(*args) if fits else general(*args)


def solution(mesh):
    tokens = P(None, ("rows", "kc"), None)
    return jax.shard_map(
        local,
        mesh=mesh,
        in_specs=(tokens,) + (P(),) * 8 + (P(None, "kc"), P(None, "rows"), tokens),
        out_specs=(tokens, tokens) + (P("rows", "kc"),) * 6 + (P("rows"), P("rows"))
        + (P("rows", "kc"),),
        check_vma=False,
    )
```
